32 devices in a mesh: grp: 4 (over x, core), dev: 8 (over z, y).
Axes of the slice: x: 2, y: 2, z: 4, core: 2. Of those that a mesh axis runs over, the one named last changes fastest.
Arguments:
- student: bfloat16 [4096, 1024], P(('grp', 'dev')), may hold values from -0.19921875 to 0.19921875
- teacher: bfloat16 [4096, 1024], P(('grp', 'dev')), may hold values from -0.19921875 to 0.19921875
- labels: int32 [4096], P(('grp', 'dev')), may hold values from 0 to 999, as said below
Outputs:
- supcon_loss: float32 [], replicated
- relation_loss: float32 [], replicated
- feature_grad: float32 [4096, 1024], P(('grp', 'dev'))
The draws below stay inside these ranges and needn't reach their ends.
Inputs may be any that keep to these rules, and one draw needn't show every extreme that they name: `labels`: each label from 875 upward belongs to exactly one view of the batch; every other view has a label below 875.
All inputs are finite; a program needn't handle non-finite values.
Results may differ from the reference program's by a relative error of at most 0.0003.
The reference program's roundings to bfloat16 on the way count: a program that leaves them out, or rounds other values in their place, can miss the bound.
Values may be sent and summed in bfloat16 or wider, within the bound.
No kernel may reach another device: no remote copies, remote signals or barrier semaphores. Data moves between devices by JAX's collectives and lax.ppermute only.
A program may use at most 128 MiB of HBM per device.

```python
import math
import jax
import jax.numpy as jnp
from jax import lax

D = 1024
CLASSES = 1000
VIEWS = 4096


def draw_labels(key, part):
    reserved = CLASSES // 8
    common_key = jax.random.fold_in(key, 11)
    place_key = jax.random.fold_in(key, 23)
    common = jax.random.randint(common_key, (VIEWS,), 0, CLASSES - reserved, dtype=jnp.int32)
    chosen = jax.random.permutation(place_key, VIEWS)[:reserved].astype(jnp.int32)
    single = CLASSES - reserved + jnp.arange(reserved, dtype=jnp.int32)
    return common.at[chosen].set(single)


def levels(key, dims, cuts, low, high):
    loudness, own = 1.0, jax.random.fold_in(key, 6)
    for position, shards_of in cuts:
        steps = jnp.exp(jax.random.uniform(jax.random.fold_in(own, position), (shards_of,), jnp.float32, low / len(cuts), high / len(cuts)))
        loudness = loudness * jnp.repeat(steps, dims[position] // shards_of).reshape([-1 if axis == position else 1 for axis in range(len(dims))])
    return loudness


def bell_draw(stream_key, extent, scale, limit, shards=(), kind=jnp.bfloat16):
    result = scale * jax.random.normal(stream_key, extent, jnp.float32)
    if shards:
        result = result * levels(stream_key, extent, shards, -0.22, 0.18)
    return jnp.clip(result, -limit, limit).astype(kind)


def setup_inputs(seed: int = 0) -> dict:
    arg_keys = jax.random.split(jax.random.key(seed), 4)
    return {
        "student": bell_draw(arg_keys[0], (VIEWS, D), 0.03125, 0.19921875, ((0, 32),)),
        "teacher": bell_draw(arg_keys[1], (VIEWS, D), 0.03125, 0.19921875, ((0, 32),)),
        "labels": draw_labels(jax.random.fold_in(arg_keys[3], 71), 0),
    }


temp_sup = 0.1
temp_student = 0.2
temp_teacher = 0.05
epsilon = 1e-06

def unit_rows(raw):
    values = raw.astype(jnp.float32)
    scaling = lax.rsqrt(lax.optimization_barrier(jnp.sum(values * values, axis=1, keepdims=True)) + epsilon)
    return (values * scaling, scaling)

def inner_rows(left, right):
    return lax.dot_general(left, right, (((1,), (1,)), ((), ())), preferred_element_type=jnp.float32)

def tile_terms(anchor_unit, anchor_teacher, anchor_label, anchor_place, key_unit, key_teacher, key_label, key_place):
    similar = inner_rows(anchor_unit, key_unit)
    teacher_sim = inner_rows(anchor_teacher, key_teacher)
    distinct = anchor_place[:, None] != key_place[None, :]
    positive = jnp.logical_and(anchor_label[:, None] == key_label[None, :], distinct).astype(jnp.float32)
    empty = jnp.zeros_like(similar)
    sup_exp = jnp.where(distinct, jnp.exp((similar - 1.0) / temp_sup), empty)
    rel_exp = jnp.where(distinct, jnp.exp((similar - 1.0) / temp_student), empty)
    teacher_exp = jnp.where(distinct, jnp.exp((teacher_sim - 1.0) / temp_teacher), empty)
    return (similar, positive, sup_exp, rel_exp, teacher_exp)

def tile_stats(terms):
    similar, positive, sup_exp, rel_exp, teacher_exp = terms
    return (lax.optimization_barrier(jnp.sum(sup_exp, axis=1)), lax.optimization_barrier(jnp.sum(rel_exp, axis=1)), lax.optimization_barrier(jnp.sum(teacher_exp, axis=1)), lax.optimization_barrier(jnp.sum(teacher_exp * similar, axis=1)), lax.optimization_barrier(jnp.sum(positive * similar, axis=1)), lax.optimization_barrier(jnp.sum(positive, axis=1)))

def coefficient(terms, sup_total, rel_total, teacher_total, positives):
    similar, positive, sup_exp, rel_exp, teacher_exp = terms
    return (sup_exp / sup_total - positive / positives) / temp_sup + (rel_exp / rel_total - teacher_exp / teacher_total) / temp_student

def row_losses(stats):
    sup_total, rel_total, teacher_total, teacher_mix, positive_sum, positive_count = stats
    positives = jnp.maximum(positive_count, 1.0)
    contrast = (1.0 - positive_sum / positives) / temp_sup + jnp.log(sup_total)
    relation = (1.0 - teacher_mix / teacher_total) / temp_student + jnp.log(rel_total)
    return (contrast, relation)

def reference(student, teacher, labels):
    view_count, width = student.shape
    unit_student, scaling = unit_rows(student)
    unit_rounded = unit_student.astype(jnp.bfloat16)
    teacher_rounded = unit_rows(teacher)[0].astype(jnp.bfloat16)
    places = jnp.arange(view_count, dtype=jnp.int32)
    block_rows = math.gcd(view_count, 512)
    block_total = view_count // block_rows
    blocked = (unit_rounded.reshape(block_total, block_rows, width), teacher_rounded.reshape(block_total, block_rows, width), labels.reshape(block_total, block_rows), places.reshape(block_total, block_rows))

    def stats_block(operands):
        return tile_stats(tile_terms(operands[0], operands[1], operands[2], operands[3], unit_rounded, teacher_rounded, labels, places))
    stats = lax.map(stats_block, blocked)
    stats = tuple((item.reshape(view_count) for item in stats))
    contrast, relation = row_losses(stats)
    coef_stats = (stats[0], stats[1], stats[2], jnp.maximum(stats[5], 1.0))
    blocked_stats = tuple((item.reshape(block_total, block_rows) for item in coef_stats))

    def grad_step(key_sum, operands):
        terms = tile_terms(operands[0], operands[1], operands[2], operands[3], unit_rounded, teacher_rounded, labels, places)
        coef = coefficient(terms, operands[4][:, None], operands[5][:, None], operands[6][:, None], operands[7][:, None]).astype(jnp.bfloat16)
        anchor_part = jnp.dot(coef, unit_rounded, preferred_element_type=jnp.float32)
        key_sum = key_sum + lax.dot_general(coef, operands[0], (((0,), (0,)), ((), ())), preferred_element_type=jnp.float32)
        return (key_sum, anchor_part)
    key_sum, anchor_parts = lax.scan(grad_step, jnp.zeros((view_count, width), jnp.float32), blocked + blocked_stats)
    grad = anchor_parts.reshape(view_count, width) + key_sum
    along = lax.optimization_barrier(jnp.sum(unit_student * grad, axis=1, keepdims=True))
    feature_grad = scaling * (grad - unit_student * along)
    return (jnp.mean(contrast), jnp.mean(relation), feature_grad)
```

```python
import functools

import jax
import jax.numpy as jnp
from jax import lax
from jax.experimental import pallas as pl
from jax.experimental.pallas import tpu as pltpu
from jax.sharding import PartitionSpec as P

temp_sup = 0.1
temp_student = 0.2
temp_teacher = 0.05
epsilon = 1e-06

AXES = ("grp", "dev")
PAD = 16
VMEM_LIMIT = 40 * 1024 * 1024


def swapped(value, axis, mask):
    size = lax.axis_size(axis)
    return lax.ppermute(value, axis, [(i, i ^ mask) for i in range(size)])


def bits_of(size):
    return [1 << i for i in range(size.bit_length() - 1)]


def unit_of(raw):
    values = raw.astype(jnp.float32)
    scaling = lax.rsqrt(jnp.sum(values * values, axis=1, keepdims=True) + epsilon)
    return (values * scaling).astype(jnp.bfloat16)


def label_row(block, rows):
    tail = block[rows : rows + PAD, 0:rows].astype(jnp.float32)
    return tail[0:1] * 256.0 + tail[1:2]


def column_of(row):
    rows = row.shape[1]
    return jnp.transpose(jnp.broadcast_to(row, (rows, rows)))


def inner_rows(left, right):
    return lax.dot_general(
        left, right, (((1,), (1,)), ((), ())), preferred_element_type=jnp.float32
    )


def call(kernel, out_shape, operands, smem=0, flops=0, name=None):
    specs = []
    for i, item in enumerate(operands):
        if i < smem:
            specs.append(pl.BlockSpec(memory_space=pltpu.SMEM))
        else:
            specs.append(pl.BlockSpec(memory_space=pltpu.VMEM))
    many = isinstance(out_shape, (tuple, list))
    out_specs = (
        tuple(pl.BlockSpec(memory_space=pltpu.VMEM) for _ in out_shape)
        if many
        else pl.BlockSpec(memory_space=pltpu.VMEM)
    )
    moved = sum(item.size * item.dtype.itemsize for item in operands)
    return pl.pallas_call(
        kernel,
        out_shape=tuple(out_shape) if many else out_shape,
        in_specs=specs,
        out_specs=out_specs,
        name=name,
        cost_estimate=pl.CostEstimate(flops=flops, bytes_accessed=moved, transcendentals=0),
        compiler_params=pltpu.CompilerParams(vmem_limit_bytes=VMEM_LIMIT),
    )(*operands)


def keys_kernel(count, rows, *refs):
    students, teachers = refs[:count], refs[count : 2 * count]
    unit_ref, teacher_ref, label_ref = refs[2 * count :]
    for k in range(count):
        place = slice(k * rows, (k + 1) * rows)
        unit_ref[place, :] = unit_of(students[k][...])
        teacher_ref[place, :] = unit_of(teachers[k][0:rows, :])
        label_ref[place, :] = column_of(label_row(teachers[k], rows))


def tile_kernel(count, rows, width, first, last, *refs):
    ids, unit_ref, teacher_ref, label_ref = refs[:4]
    students, teachers = refs[4:6], refs[6:8]
    rest = refs[8:]
    if not first:
        old_ref, rest = rest[0], rest[1:]
    anchor_ref, similar_ref, weight_ref, anchor_label_ref, stats_ref = rest[:5]
    teacher_units = []
    for n in range(2):
        anchor_ref[n * rows : (n + 1) * rows, :] = unit_of(students[n][...])
        teacher_units.append(unit_of(teachers[n][0:rows, :]))
        anchor_label_ref[:, n * rows : (n + 1) * rows] = jnp.broadcast_to(
            label_row(teachers[n], rows), (8, rows)
        )
    similar_ref[...] = inner_rows(unit_ref[...], anchor_ref[...])
    weight_ref[...] = inner_rows(teacher_ref[...], jnp.concatenate(teacher_units, axis=0))
    row_at = lax.broadcasted_iota(jnp.int32, (rows, rows), 0)
    lane_at = lax.broadcasted_iota(jnp.int32, (rows, rows), 1)
    for k in range(count):
        down = slice(k * rows, (k + 1) * rows)
        totals = [jnp.zeros((rows, rows), jnp.float32)] * 6
        for n in range(2):
            across = slice(n * rows, (n + 1) * rows)
            similar = similar_ref[down, across]
            offset = jnp.where(ids[k] == ids[count + n], 0, rows)
            distinct = row_at != lane_at - offset
            rel_exp = jnp.where(distinct, jnp.exp((similar - 1.0) / temp_student), 0.0)
            weight = jnp.where(
                distinct, jnp.exp((weight_ref[down, across] - 1.0) / temp_teacher), 0.0
            )
            weight_ref[down, across] = weight
            same = label_ref[down, :] == anchor_label_ref[0:1, across]
            positive = jnp.where(jnp.logical_and(same, distinct), 1.0, 0.0)
            terms = (
                rel_exp * rel_exp,
                rel_exp,
                weight,
                weight * similar,
                positive * similar,
                positive,
            )
            totals = [total + term for total, term in zip(totals, terms)]
        stats = jnp.zeros((rows, rows), jnp.float32)
        for i, total in enumerate(totals):
            stats = jnp.where(lane_at == i, jnp.sum(total, axis=1, keepdims=True), stats)
        if not first:
            stats = stats + old_ref[down, :]
        stats_ref[down, :] = stats
        if last:
            rest[5][:, down] = jnp.transpose(stats)[0:8, :]


def merge_kernel(dims, rows, *refs):
    groups, members, keys, pair_places = dims
    place, received_ref, own_ref = refs[:3]
    others = refs[3 : 2 + keys]
    anchor_ref, key_ref, loss_ref = refs[2 + keys :]
    c, p, q, r = place[0], place[1], place[2], place[3]
    quarter = members // 4
    for k in range(keys):
        total = own_ref[:, k * rows : (k + 1) * rows]
        for m, other in enumerate(others):
            at = (k ^ (m + 1)) * rows
            total = total + other[:, at : at + rows]
        positives = jnp.maximum(total[5:6], 1.0)
        if k == 0:
            contrast = (1.0 - total[4:5] / positives) / temp_sup + jnp.log(total[0:1])
            relation = (1.0 - total[3:4] / total[2:3]) / temp_student + jnp.log(total[1:2])
            both = jnp.concatenate([contrast, relation] + [jnp.zeros((6, rows), jnp.float32)], axis=0)
            loss_ref[...] = jnp.broadcast_to(jnp.sum(both, axis=1, keepdims=True), (8, rows))
        factors = jnp.concatenate(
            [
                (1.0 / temp_sup) / total[0:1],
                (1.0 / temp_student) / total[1:2],
                (1.0 / temp_student) / total[2:3],
                (1.0 / temp_sup) / positives,
                jnp.zeros((rows - 4, rows), jnp.float32),
            ],
            axis=0,
        )
        key_ref[k * rows : (k + 1) * rows, :] = jnp.transpose(factors)
    low = lax.broadcasted_iota(jnp.int32, (8, rows), 0)
    for i in range(quarter):
        for dc in range(2):
            total = jnp.zeros((8, rows), jnp.float32)
            for h in range(groups // 2):
                for qq in range(2):
                    source = (h * 2 + (c ^ dc)) * members + (q * 2 + qq) * quarter + (r ^ i)
                    total = total + received_ref[pl.ds(pl.multiple_of(source * 8, 8), 8), :]
            kind = low & 3
            factors = jnp.where(
                kind == 3,
                (1.0 / temp_sup) / jnp.maximum(total, 1.0),
                jnp.where(kind == 0, 1.0 / temp_sup, 1.0 / temp_student) / total,
            )
            turned = jnp.concatenate([factors[4:8], factors[0:4]], axis=0)
            near = jnp.where(p == 0, factors, turned)
            far = jnp.where(p == 0, turned, factors)
            for slot, value in enumerate((near, far)):
                at = ((i * 2 + slot) * 2 + dc) * rows
                anchor_ref[:, at : at + rows] = value


def grad_kernel(pairs, rows, width, k, count, *refs):
    ids, label_ref, key_ref, anchor_stats_ref = refs[:4]
    rest = refs[4:]
    similar, weights, labels, units = (rest[i * pairs : (i + 1) * pairs] for i in range(4))
    out_ref = rest[4 * pairs]
    down = slice(k * rows, (k + 1) * rows)
    row_at = lax.broadcasted_iota(jnp.int32, (rows, rows), 0)
    lane_at = lax.broadcasted_iota(jnp.int32, (rows, rows), 1)
    sup_key, rel_key, teacher_key, pos_key = (key_ref[down, i : i + 1] for i in range(4))
    total = None
    for i in range(pairs):
        row_parts, column_parts = [], []
        for n in range(2):
            across = slice(n * rows, (n + 1) * rows)
            at = (i * 2 + n) * rows
            sup_all, rel_all, teacher_all, pos_all = (
                anchor_stats_ref[j : j + 1, at : at + rows] for j in range(4)
            )
            offset = jnp.where(ids[k] == ids[count + i * 2 + n], 0, rows)
            distinct = row_at != lane_at - offset
            rel_exp = jnp.where(
                distinct, jnp.exp((similar[i][down, across] - 1.0) / temp_student), 0.0
            )
            sup_exp = rel_exp * rel_exp
            weight = weights[i][down, across]
            same = label_ref[down, :] == labels[i][0:1, across]
            positive = jnp.where(jnp.logical_and(same, distinct), 1.0, 0.0)
            row_parts.append(
                (
                    (sup_exp * sup_key - positive * pos_key)
                    + (rel_exp * rel_key - weight * teacher_key)
                ).astype(jnp.bfloat16)
            )
            column_parts.append(
                (
                    (sup_exp * sup_all - positive * pos_all)
                    + (rel_exp * rel_all - weight * teacher_all)
                ).astype(jnp.bfloat16)
            )
        both = jnp.concatenate(
            [jnp.concatenate(row_parts, axis=1), jnp.concatenate(column_parts, axis=1)], axis=0
        )
        part = jnp.dot(both, units[i][...], preferred_element_type=jnp.float32)
        total = part if total is None else total + part
    out_ref[...] = total[0:rows] + total[rows : 2 * rows]


def final_kernel(student_ref, *refs):
    out_ref = refs[-1]
    grad = refs[0][...]
    for ref in refs[1:-1]:
        grad = grad + ref[...]
    values = student_ref[...].astype(jnp.float32)
    scaling = lax.rsqrt(jnp.sum(values * values, axis=1, keepdims=True) + epsilon)
    unit = values * scaling
    along = jnp.sum(unit * grad, axis=1, keepdims=True)
    out_ref[...] = scaling * (grad - unit * along)


def by_xor(value, axis, index):
    for bit in bits_of(value.shape[axis]):
        order = [i ^ bit for i in range(value.shape[axis])]
        turned = jnp.concatenate([lax.slice_in_dim(value, i, i + 1, axis=axis) for i in order], axis=axis)
        value = jnp.where((index & bit) != 0, turned, value)
    return value


def body(student, teacher, labels):
    rows, width = student.shape
    groups, members = lax.axis_size("grp"), lax.axis_size("dev")
    halves, quarter = groups // 2, members // 4
    group, member = lax.axis_index("grp"), lax.axis_index("dev")
    h, c = group // 2, group % 2
    p, q, r = member // (2 * quarter), (member // quarter) % 2, member % quarter
    inner = p != q
    cross = [
        (d, d ^ (3 * quarter)) for d in range(members) if (d // (2 * quarter)) != (d // quarter) % 2
    ]

    digits = jnp.stack([labels // 256, labels % 256]).astype(jnp.bfloat16)
    tail = jnp.pad(digits, ((0, PAD - 2), (0, width - rows)))
    own = (student, jnp.concatenate([teacher, tail], axis=0))

    def both(move, block):
        return tuple(move(part) for part in block)

    near = both(lambda v: swapped(v, "dev", quarter), own)
    crossed = both(lambda v: lax.ppermute(v, "dev", cross), own)
    keys = [own, near]
    for bit in bits_of(halves):
        keys = keys + [both(lambda v: swapped(v, "grp", 2 * bit), item) for item in keys]
    far = both(lambda v: lax.ppermute(v, "dev", cross), near)
    anchors = [
        tuple(jnp.where(inner, a, b) for a, b in zip(crossed, own)),
        tuple(jnp.where(inner, a, b) for a, b in zip(far, near)),
    ]
    for bit in bits_of(quarter):
        anchors = anchors + [both(lambda v: swapped(v, "dev", bit), item) for item in anchors]
    pairs = [(item, both(lambda v: swapped(v, "grp", 1), item)) for item in anchors]

    key_count, pair_count = len(keys), len(pairs)
    key_rows = key_count * rows
    key_ids = [
        ((h ^ (k // 2)) * 2 + c) * members + (p * 2 + (q ^ (k % 2))) * quarter + r
        for k in range(key_count)
    ]
    anchor_ids = [
        (h * 2 + (c ^ dc)) * members + (q * 2 + (p ^ (i % 2))) * quarter + (r ^ (i // 2))
        for i in range(pair_count)
        for dc in range(2)
    ]
    ids = jnp.stack(key_ids + anchor_ids).astype(jnp.int32)
    f32 = functools.partial(jax.ShapeDtypeStruct, dtype=jnp.float32)
    b16 = functools.partial(jax.ShapeDtypeStruct, dtype=jnp.bfloat16)

    key_unit, key_teacher, key_label = call(
        functools.partial(keys_kernel, key_count, rows),
        (b16((key_rows, width)), b16((key_rows, width)), f32((key_rows, rows))),
        [k[0] for k in keys] + [k[1] for k in keys],
        flops=8 * key_rows * width,
        name="keys",
    )
    units, similar, weights, anchor_labels = [], [], [], []
    stats = None
    for i, (first, second) in enumerate(pairs):
        last = i == pair_count - 1
        tile_ids = jnp.concatenate([ids[:key_count], ids[key_count + 2 * i : key_count + 2 * i + 2]])
        outs = call(
            functools.partial(tile_kernel, key_count, rows, width, stats is None, last),
            (
                b16((2 * rows, width)),
                f32((key_rows, 2 * rows)),
                f32((key_rows, 2 * rows)),
                f32((8, 2 * rows)),
                f32((key_rows, rows)),
            )
            + ((f32((8, key_rows)),) if last else ()),
            [tile_ids, key_unit, key_teacher, key_label, first[0], second[0], first[1], second[1]]
            + ([] if stats is None else [stats]),
            smem=1,
            flops=8 * key_rows * rows * width,
            name="tile",
        )
        for held, value in zip((units, similar, weights, anchor_labels), outs[:4]):
            held.append(value)
        stats = outs[4]
    sums = outs[5]

    others = []
    for k in range(1, key_count):
        mask = (k // 2) * 2 * members + (k % 2) * quarter
        total = groups * members
        others.append(lax.ppermute(sums, AXES, [(i, i ^ mask) for i in range(total)]))
    blocks = jnp.stack([sums[0], sums[1], sums[2], sums[5]]).reshape(4, halves, 2, rows)
    blocks = by_xor(by_xor(blocks, 1, h), 2, q).transpose(1, 2, 0, 3).reshape(halves, 1, 8, rows)
    payload = jnp.broadcast_to(blocks, (halves, 2 * members, 8, rows)).reshape(-1, rows)
    received = lax.all_to_all(payload, AXES, 0, 0, tiled=True)
    anchor_stats, key_stats, loss = call(
        functools.partial(merge_kernel, (groups, members, key_count, pair_count), rows),
        (f32((8, members * rows)), f32((key_rows, rows)), f32((8, rows))),
        [jnp.stack([c, p, q, r]).astype(jnp.int32), received, sums] + others,
        smem=1,
        name="merge",
    )

    def grads(k):
        operands = [ids, key_label, key_stats, anchor_stats] + similar + weights + anchor_labels + units
        return call(
            functools.partial(grad_kernel, pair_count, rows, width, k, key_count),
            f32((rows, width)),
            operands,
            smem=1,
            flops=4 * rows * members * rows * width,
            name="grads",
        )

    parts = []
    for k in range(key_count - 1, -1, -1):
        part = grads(k)
        if k:
            mask = (k // 2) * 2 * members + (k % 2) * quarter
            part = lax.ppermute(part, AXES, [(i, i ^ mask) for i in range(groups * members)])
        parts.append(part)
    shared = lax.all_to_all(
        jnp.broadcast_to(loss[None], (groups * members, 8, rows)).reshape(-1, rows), AXES, 0, 0, tiled=True
    ).reshape(groups * members, 8, rows)
    losses = jnp.sum(shared[:, 0:2, 0], axis=0) / (groups * members * rows)
    feature_grad = call(
        final_kernel, f32((rows, width)), [student] + parts[::-1], flops=8 * rows * width, name="final"
    )
    return (losses[0], losses[1], feature_grad)


def solution(mesh):
    placed = (P(AXES, None), P(AXES, None), P(AXES))
    return jax.shard_map(
        body,
        mesh=mesh,
        in_specs=placed,
        out_specs=(P(), P(), P(AXES, None)),
        check_vma=False,
    )
```

```python
import functools

import jax
import jax.numpy as jnp
from jax import lax
from jax.experimental import pallas as pl
from jax.experimental.pallas import tpu as pltpu
from jax.sharding import PartitionSpec as P

temp_sup = 0.1
temp_student = 0.2
temp_teacher = 0.05
epsilon = 1e-06

AXES = ("grp", "dev")
EARLY = 2
PAD = 16
VMEM_LIMIT = 63 * 1024 * 1024


def swapped(value, axis, mask):
    size = lax.axis_size(axis)
    return lax.ppermute(value, axis, [(i, i ^ mask) for i in range(size)])


def bits_of(size):
    return [1 << i for i in range(size.bit_length() - 1)]


def unit_of(raw):
    values = raw.astype(jnp.float32)
    scaling = lax.rsqrt(jnp.sum(values * values, axis=1, keepdims=True) + epsilon)
    return (values * scaling).astype(jnp.bfloat16)


def label_row(block, rows):
    tail = block[rows : rows + PAD, 0:rows].astype(jnp.float32)
    return tail[0:1] * 256.0 + tail[1:2]


def column_of(row):
    rows = row.shape[1]
    return jnp.transpose(jnp.broadcast_to(row, (rows, rows)))


def inner_rows(left, right):
    return lax.dot_general(
        left, right, (((1,), (1,)), ((), ())), preferred_element_type=jnp.float32
    )


def call(kernel, out_shape, operands, flops=0, name=None, blocks=None):
    specs = []
    for i, item in enumerate(operands):
        size, at = (blocks or {}).get(i, (item.shape[0], 0))
        specs.append(
            pl.BlockSpec((size, item.shape[1]), functools.partial(lambda at, step: (at, 0), at))
        )
    many = isinstance(out_shape, (tuple, list))
    outs = tuple(out_shape) if many else (out_shape,)
    out_specs = tuple(pl.BlockSpec(item.shape, lambda step: (0, 0)) for item in outs)
    moved = sum(item.size * item.dtype.itemsize for item in operands)
    return pl.pallas_call(
        kernel,
        out_shape=outs if many else out_shape,
        grid=(1,),
        in_specs=specs,
        out_specs=out_specs if many else out_specs[0],
        name=name,
        cost_estimate=pl.CostEstimate(flops=flops, bytes_accessed=moved, transcendentals=0),
        compiler_params=pltpu.CompilerParams(vmem_limit_bytes=VMEM_LIMIT),
    )(*operands)


def place():
    group, member = lax.axis_index("grp"), lax.axis_index("dev")
    quarter = lax.axis_size("dev") // 4
    return (
        group // 2,
        group % 2,
        member // (2 * quarter),
        (member // quarter) % 2,
        member % quarter,
    )


def key_id(k):
    h, c, p, q, r = place()
    members = lax.axis_size("dev")
    return ((h ^ (k // 2)) * 2 + c) * members + (p * 2 + (q ^ (k % 2))) * (members // 4) + r


def anchor_id(i, dc):
    h, c, p, q, r = place()
    members = lax.axis_size("dev")
    return (h * 2 + (c ^ dc)) * members + (q * 2 + (p ^ (i % 2))) * (members // 4) + (r ^ (i // 2))


def keys_kernel(count, rows, *refs):
    students, teachers = refs[:count], refs[count : 2 * count]
    unit_ref, teacher_ref, label_ref = refs[2 * count :]
    for k in range(count):
        place = slice(k * rows, (k + 1) * rows)
        unit_ref[place, :] = unit_of(students[k][...])
        teacher_ref[place, :] = unit_of(teachers[k][0:rows, :])
        label_ref[place, :] = column_of(label_row(teachers[k], rows))


def tile_kernel(count, rows, i, last, *refs):
    unit_ref, teacher_ref, label_ref = refs[:3]
    students, teachers = refs[3:5], refs[5:7]
    rest = refs[7:]
    first = i == 0
    if not first:
        old_ref, rest = rest[0], rest[1:]
    anchor_ref, similar_ref, weight_ref, anchor_label_ref, stats_ref = rest[:5]
    teacher_units = []
    for n in range(2):
        anchor_ref[n * rows : (n + 1) * rows, :] = unit_of(students[n][...])
        teacher_units.append(unit_of(teachers[n][0:rows, :]))
        anchor_label_ref[:, n * rows : (n + 1) * rows] = jnp.broadcast_to(
            label_row(teachers[n], rows), (8, rows)
        )
    similar_ref[...] = inner_rows(unit_ref[...], anchor_ref[...])
    weight_ref[...] = inner_rows(teacher_ref[...], jnp.concatenate(teacher_units, axis=0))
    row_at = lax.broadcasted_iota(jnp.int32, (rows, rows), 0)
    lane_at = lax.broadcasted_iota(jnp.int32, (rows, rows), 1)
    for k in range(count):
        down = slice(k * rows, (k + 1) * rows)
        totals = [jnp.zeros((rows, rows), jnp.float32)] * 6
        for n in range(2):
            across = slice(n * rows, (n + 1) * rows)
            similar = similar_ref[down, across]
            offset = jnp.where(key_id(k) == anchor_id(i, n), 0, rows)
            distinct = row_at != lane_at - offset
            rel_exp = jnp.where(distinct, jnp.exp((similar - 1.0) / temp_student), 0.0)
            weight = jnp.where(
                distinct, jnp.exp((weight_ref[down, across] - 1.0) / temp_teacher), 0.0
            )
            weight_ref[down, across] = weight
            same = label_ref[down, :] == anchor_label_ref[0:1, across]
            positive = jnp.where(jnp.logical_and(same, distinct), 1.0, 0.0)
            terms = (
                rel_exp * rel_exp,
                rel_exp,
                weight,
                weight * similar,
                positive * similar,
                positive,
            )
            totals = [total + term for total, term in zip(totals, terms)]
        stats = jnp.zeros((rows, rows), jnp.float32)
        for j, total in enumerate(totals):
            stats = jnp.where(lane_at == j, jnp.sum(total, axis=1, keepdims=True), stats)
        if not first:
            stats = stats + old_ref[down, :]
        stats_ref[down, :] = stats
        if last:
            rest[5][:, down] = jnp.transpose(stats)[0:8, :]


def merge_kernel(dims, rows, *refs):
    groups, members, keys = dims
    received_ref, own_ref = refs[:2]
    others = refs[2 : 1 + keys]
    anchor_ref, key_ref, loss_ref = refs[1 + keys :]
    _, c, p, q, r = place()
    quarter = members // 4
    for k in range(keys):
        total = own_ref[:, k * rows : (k + 1) * rows]
        for m, other in enumerate(others):
            at = (k ^ (m + 1)) * rows
            total = total + other[:, at : at + rows]
        positives = jnp.maximum(total[5:6], 1.0)
        if k == 0:
            contrast = (1.0 - total[4:5] / positives) / temp_sup + jnp.log(total[0:1])
            relation = (1.0 - total[3:4] / total[2:3]) / temp_student + jnp.log(total[1:2])
            both = jnp.concatenate([contrast, relation] + [jnp.zeros((6, rows), jnp.float32)], axis=0)
            loss_ref[...] = jnp.broadcast_to(jnp.sum(both, axis=1, keepdims=True), (8, rows))
        factors = jnp.concatenate(
            [
                (1.0 / temp_sup) / total[0:1],
                (1.0 / temp_student) / total[1:2],
                (1.0 / temp_student) / total[2:3],
                (1.0 / temp_sup) / positives,
                jnp.zeros((rows - 4, rows), jnp.float32),
            ],
            axis=0,
        )
        key_ref[k * rows : (k + 1) * rows, :] = jnp.transpose(factors)
    low = lax.broadcasted_iota(jnp.int32, (8, rows), 0)
    for i in range(quarter):
        for dc in range(2):
            total = jnp.zeros((8, rows), jnp.float32)
            for h in range(groups // 2):
                for qq in range(2):
                    source = (h * 2 + (c ^ dc)) * members + (q * 2 + qq) * quarter + (r ^ i)
                    total = total + received_ref[pl.ds(pl.multiple_of(source * 8, 8), 8), :]
            kind = low & 3
            factors = jnp.where(
                kind == 3,
                (1.0 / temp_sup) / jnp.maximum(total, 1.0),
                jnp.where(kind == 0, 1.0 / temp_sup, 1.0 / temp_student) / total,
            )
            turned = jnp.concatenate([factors[4:8], factors[0:4]], axis=0)
            near = jnp.where(p == 0, factors, turned)
            far = jnp.where(p == 0, turned, factors)
            for slot, value in enumerate((near, far)):
                at = ((i * 2 + slot) * 2 + dc) * rows
                anchor_ref[:, at : at + rows] = value


def grad_kernel(pairs, rows, k, *refs):
    label_ref, key_ref, anchor_stats_ref = refs[:3]
    rest = refs[3:]
    similar, weights, labels, units = (rest[i * pairs : (i + 1) * pairs] for i in range(4))
    out_ref = rest[4 * pairs]
    row_at = lax.broadcasted_iota(jnp.int32, (rows, rows), 0)
    lane_at = lax.broadcasted_iota(jnp.int32, (rows, rows), 1)
    sup_key, rel_key, teacher_key, pos_key = (key_ref[:, i : i + 1] for i in range(4))
    total = None
    for i in range(pairs):
        row_parts, column_parts = [], []
        for n in range(2):
            across = slice(n * rows, (n + 1) * rows)
            at = (i * 2 + n) * rows
            sup_all, rel_all, teacher_all, pos_all = (
                anchor_stats_ref[j : j + 1, at : at + rows] for j in range(4)
            )
            offset = jnp.where(key_id(k) == anchor_id(i, n), 0, rows)
            distinct = row_at != lane_at - offset
            rel_exp = jnp.where(
                distinct, jnp.exp((similar[i][:, across] - 1.0) / temp_student), 0.0
            )
            sup_exp = rel_exp * rel_exp
            weight = weights[i][:, across]
            same = label_ref[...] == labels[i][0:1, across]
            positive = jnp.where(jnp.logical_and(same, distinct), 1.0, 0.0)
            row_parts.append(
                (
                    (sup_exp * sup_key - positive * pos_key)
                    + (rel_exp * rel_key - weight * teacher_key)
                ).astype(jnp.bfloat16)
            )
            column_parts.append(
                (
                    (sup_exp * sup_all - positive * pos_all)
                    + (rel_exp * rel_all - weight * teacher_all)
                ).astype(jnp.bfloat16)
            )
        both = jnp.concatenate(
            [jnp.concatenate(row_parts, axis=1), jnp.concatenate(column_parts, axis=1)], axis=0
        )
        part = jnp.dot(both, units[i][...], preferred_element_type=jnp.float32)
        total = part if total is None else total + part
    out_ref[...] = total[0:rows] + total[rows : 2 * rows]


def final_kernel(student_ref, *refs):
    out_ref = refs[-1]
    grad = refs[0][...]
    for ref in refs[1:-1]:
        grad = grad + ref[...]
    values = student_ref[...].astype(jnp.float32)
    scaling = lax.rsqrt(jnp.sum(values * values, axis=1, keepdims=True) + epsilon)
    unit = values * scaling
    along = jnp.sum(unit * grad, axis=1, keepdims=True)
    out_ref[...] = scaling * (grad - unit * along)


def by_xor(value, axis, index):
    for bit in bits_of(value.shape[axis]):
        order = [i ^ bit for i in range(value.shape[axis])]
        turned = jnp.concatenate([lax.slice_in_dim(value, i, i + 1, axis=axis) for i in order], axis=axis)
        value = jnp.where((index & bit) != 0, turned, value)
    return value


def body(student, teacher, labels):
    rows, width = student.shape
    groups, members = lax.axis_size("grp"), lax.axis_size("dev")
    halves, quarter = groups // 2, members // 4
    h, c, p, q, r = place()
    inner = p != q
    cross = [
        (d, d ^ (3 * quarter)) for d in range(members) if (d // (2 * quarter)) != (d // quarter) % 2
    ]

    digits = jnp.stack([labels // 256, labels % 256]).astype(jnp.bfloat16)
    tail = jnp.pad(digits, ((0, PAD - 2), (0, width - rows)))
    own = (student, jnp.concatenate([teacher, tail], axis=0))

    def both(move, block):
        return tuple(move(part) for part in block)

    near = both(lambda v: swapped(v, "dev", quarter), own)
    crossed = both(lambda v: lax.ppermute(v, "dev", cross), own)
    keys = [own, near]
    for bit in bits_of(halves):
        keys = keys + [both(lambda v: swapped(v, "grp", 2 * bit), item) for item in keys]
    far = both(lambda v: lax.ppermute(v, "dev", cross), near)
    anchors = [
        tuple(jnp.where(inner, a, b) for a, b in zip(crossed, own)),
        tuple(jnp.where(inner, a, b) for a, b in zip(far, near)),
    ]
    for bit in bits_of(quarter):
        anchors = anchors + [both(lambda v: swapped(v, "dev", bit), item) for item in anchors]
    late = len(anchors) - 1
    pairs = [(item, both(lambda v: swapped(v, "grp", 1), item)) for item in anchors[:late]]

    key_count, pair_count = len(keys), len(anchors)
    key_rows = key_count * rows
    f32 = functools.partial(jax.ShapeDtypeStruct, dtype=jnp.float32)
    b16 = functools.partial(jax.ShapeDtypeStruct, dtype=jnp.bfloat16)

    key_unit, key_teacher, key_label = call(
        functools.partial(keys_kernel, key_count, rows),
        (b16((key_rows, width)), b16((key_rows, width)), f32((key_rows, rows))),
        [k[0] for k in keys] + [k[1] for k in keys],
        flops=8 * key_rows * width,
        name="keys",
    )
    units, similar, weights, anchor_labels = [], [], [], []
    stats = None
    for i in range(pair_count):
        last = i == pair_count - 1
        if i == EARLY:
            held_stats, anchors[late] = lax.optimization_barrier((stats, anchors[late]))
            stats = held_stats
            pairs.append((anchors[late], both(lambda v: swapped(v, "grp", 1), anchors[late])))
        first, second = pairs[i]
        outs = call(
            functools.partial(tile_kernel, key_count, rows, i, last),
            (
                b16((2 * rows, width)),
                f32((key_rows, 2 * rows)),
                f32((key_rows, 2 * rows)),
                f32((8, 2 * rows)),
                f32((key_rows, rows)),
            )
            + ((f32((8, key_rows)),) if last else ()),
            [key_unit, key_teacher, key_label, first[0], second[0], first[1], second[1]]
            + ([] if stats is None else [stats]),
            flops=8 * key_rows * rows * width,
            name="tile",
        )
        for held, value in zip((units, similar, weights, anchor_labels), outs[:4]):
            held.append(value)
        stats = outs[4]
    sums = outs[5]

    others = []
    for k in range(1, key_count):
        mask = (k // 2) * 2 * members + (k % 2) * quarter
        total = groups * members
        others.append(lax.ppermute(sums, AXES, [(i, i ^ mask) for i in range(total)]))
    blocks = jnp.stack([sums[0], sums[1], sums[2], sums[5]]).reshape(4, halves, 2, rows)
    blocks = by_xor(by_xor(blocks, 1, h), 2, q).transpose(1, 2, 0, 3).reshape(halves, 1, 8, rows)
    payload = jnp.broadcast_to(blocks, (halves, 2 * members, 8, rows)).reshape(-1, rows)
    received = lax.all_to_all(payload, AXES, 0, 0, tiled=True)
    anchor_stats, key_stats, loss = call(
        functools.partial(merge_kernel, (groups, members, key_count), rows),
        (f32((8, members * rows)), f32((key_rows, rows)), f32((8, rows))),
        [received, sums] + others,
        name="merge",
    )

    def grads(k, key_stats):
        blocks = {i: (rows, k) for i in (0, 1)}
        for i in range(2 * pair_count):
            blocks[3 + i] = (rows, k)
        operands = [key_label, key_stats, anchor_stats] + similar + weights + anchor_labels + units
        return call(
            functools.partial(grad_kernel, pair_count, rows, k),
            f32((rows, width)),
            operands,
            flops=4 * rows * members * rows * width,
            name="grads",
            blocks=blocks,
        )

    parts = []
    for k in range(key_count - 1, -1, -1):
        part = grads(k, key_stats)
        if k:
            key_stats, part = lax.optimization_barrier((key_stats, part))
            mask = (k // 2) * 2 * members + (k % 2) * quarter
            part = lax.ppermute(part, AXES, [(i, i ^ mask) for i in range(groups * members)])
        parts.append(part)
    loss, parts[0], parts[-1] = lax.optimization_barrier((loss, parts[0], parts[-1]))
    shared = lax.all_to_all(
        jnp.broadcast_to(loss[None], (groups * members, 8, rows)).reshape(-1, rows), AXES, 0, 0, tiled=True
    ).reshape(groups * members, 8, rows)
    losses = jnp.sum(shared[:, 0:2, 0], axis=0) / (groups * members * rows)
    feature_grad = call(
        final_kernel, f32((rows, width)), [student] + parts[::-1], flops=8 * rows * width, name="final"
    )
    return (losses[0], losses[1], feature_grad)


def solution(mesh):
    placed = (P(AXES, None), P(AXES, None), P(AXES))
    return jax.shard_map(
        body,
        mesh=mesh,
        in_specs=placed,
        out_specs=(P(), P(), P(AXES, None)),
        check_vma=False,
    )
```

```python
import functools

import jax
import jax.numpy as jnp
from jax import lax
from jax.experimental import pallas as pl
from jax.experimental.pallas import tpu as pltpu
from jax.sharding import PartitionSpec as P

temp_sup = 0.1
temp_student = 0.2
temp_teacher = 0.05
epsilon = 1e-06

AXES = ("grp", "dev")
GROUP = 2
PAD = 16
VMEM_LIMIT = 63 * 1024 * 1024


def swapped(value, axis, mask):
    size = lax.axis_size(axis)
    return lax.ppermute(value, axis, [(i, i ^ mask) for i in range(size)])


def bits_of(size):
    return [1 << i for i in range(size.bit_length() - 1)]


def unit_of(raw):
    values = raw.astype(jnp.float32)
    scaling = lax.rsqrt(jnp.sum(values * values, axis=1, keepdims=True) + epsilon)
    return (values * scaling).astype(jnp.bfloat16)


def label_row(block, rows):
    tail = block[rows : rows + PAD, 0:rows].astype(jnp.float32)
    return tail[0:1] * 256.0 + tail[1:2]


def column_of(row):
    rows = row.shape[1]
    return jnp.transpose(jnp.broadcast_to(row, (rows, rows)))


def inner_rows(left, right):
    return lax.dot_general(
        left, right, (((1,), (1,)), ((), ())), preferred_element_type=jnp.float32
    )


def call(kernel, out_shape, operands, flops=0, name=None, blocks=None):
    def spec(shape, given):
        if given is None:
            return pl.BlockSpec(shape, lambda step: (0, 0))
        return pl.BlockSpec(*given)

    many = isinstance(out_shape, (tuple, list))
    shapes = tuple(out_shape) if many else (out_shape,)
    out_specs = tuple(spec(item.shape, None) for item in shapes)
    moved = sum(item.size * item.dtype.itemsize for item in operands)
    return pl.pallas_call(
        kernel,
        out_shape=shapes if many else out_shape,
        grid=(1,),
        in_specs=[spec(item.shape, (blocks or {}).get(i)) for i, item in enumerate(operands)],
        out_specs=out_specs if many else out_specs[0],
        name=name,
        cost_estimate=pl.CostEstimate(flops=flops, bytes_accessed=moved, transcendentals=0),
        compiler_params=pltpu.CompilerParams(vmem_limit_bytes=VMEM_LIMIT),
    )(*operands)


def place():
    group, member = lax.axis_index("grp"), lax.axis_index("dev")
    quarter = lax.axis_size("dev") // 4
    return (
        group // 2,
        group % 2,
        member // (2 * quarter),
        (member // quarter) % 2,
        member % quarter,
    )


def key_id(k):
    h, c, p, q, r = place()
    members = lax.axis_size("dev")
    return ((h ^ (k // 2)) * 2 + c) * members + (p * 2 + (q ^ (k % 2))) * (members // 4) + r


def anchor_id(i, dc):
    h, c, p, q, r = place()
    members = lax.axis_size("dev")
    return (h * 2 + (c ^ dc)) * members + (q * 2 + (p ^ (i % 2))) * (members // 4) + (r ^ (i // 2))


def keys_kernel(count, rows, *refs):
    students, teachers = refs[:count], refs[count : 2 * count]
    unit_ref, teacher_ref, label_ref = refs[2 * count :]
    for k in range(count):
        place = slice(k * rows, (k + 1) * rows)
        unit_ref[place, :] = unit_of(students[k][...])
        teacher_ref[place, :] = unit_of(teachers[k][0:rows, :])
        label_ref[place, :] = column_of(label_row(teachers[k], rows))


def tile_kernel(count, rows, i, n_blocks, last, *refs):
    unit_ref, teacher_ref, label_ref = refs[:3]
    students, teachers = refs[3 : 3 + n_blocks], refs[3 + n_blocks : 3 + 2 * n_blocks]
    rest = refs[3 + 2 * n_blocks :]
    first = i == 0
    if not first:
        old_ref, rest = rest[0], rest[1:]
    anchor_ref, similar_ref, weight_ref, anchor_label_ref, stats_ref = rest[:5]
    teacher_units = []
    for n in range(n_blocks):
        across = slice(n * rows, (n + 1) * rows)
        anchor_ref[across, :] = unit_of(students[n][...])
        teacher_units.append(unit_of(teachers[n][0:rows, :]))
        anchor_label_ref[:, across] = jnp.broadcast_to(label_row(teachers[n], rows), (8, rows))
    similar_ref[...] = inner_rows(unit_ref[...], anchor_ref[...])
    weight_ref[...] = inner_rows(teacher_ref[...], jnp.concatenate(teacher_units, axis=0))
    row_at = lax.broadcasted_iota(jnp.int32, (rows, rows), 0)
    lane_at = lax.broadcasted_iota(jnp.int32, (rows, rows), 1)
    for k in range(count):
        down = slice(k * rows, (k + 1) * rows)
        totals = [jnp.zeros((rows, rows), jnp.float32)] * 6
        for n in range(n_blocks):
            across = slice(n * rows, (n + 1) * rows)
            similar = similar_ref[down, across]
            same_block = key_id(k) == anchor_id((i * n_blocks + n) // 2, n % 2)
            distinct = row_at != lane_at - jnp.where(same_block, 0, rows)
            rel_exp = jnp.where(distinct, jnp.exp((similar - 1.0) / temp_student), 0.0)
            weight = jnp.where(
                distinct, jnp.exp((weight_ref[down, across] - 1.0) / temp_teacher), 0.0
            )
            weight_ref[down, across] = weight
            same = label_ref[down, :] == anchor_label_ref[0:1, across]
            positive = jnp.where(jnp.logical_and(same, distinct), 1.0, 0.0)
            terms = (
                rel_exp * rel_exp,
                rel_exp,
                weight,
                weight * similar,
                positive * similar,
                positive,
            )
            totals = [total + term for total, term in zip(totals, terms)]
        stats = jnp.zeros((rows, rows), jnp.float32)
        for j, total in enumerate(totals):
            stats = jnp.where(lane_at == j, jnp.sum(total, axis=1, keepdims=True), stats)
        if not first:
            stats = stats + old_ref[down, :]
        stats_ref[down, :] = stats
        if last:
            rest[5][:, down] = jnp.transpose(stats)[0:8, :]


def payload_kernel(halves, members, rows, sums_ref, out_ref):
    h, _, _, q, _ = place()
    for half in range(halves):
        both = []
        for other in range(2):
            block = (half ^ h) * 2 + (other ^ q)
            values = sums_ref[:, pl.ds(pl.multiple_of(block * rows, rows), rows)]
            both += [values[0:3], values[5:6]]
        tile = jnp.concatenate(both, axis=0)
        for d in range(2 * members):
            at = (half * 2 * members + d) * 8
            out_ref[at : at + 8, :] = tile


def merge_kernel(dims, rows, *refs):
    groups, members, keys = dims
    received_ref, own_ref = refs[:2]
    others = refs[2 : 1 + keys]
    anchor_ref, key_ref, loss_ref = refs[1 + keys :]
    _, c, p, q, r = place()
    quarter = members // 4
    for k in range(keys):
        total = own_ref[:, k * rows : (k + 1) * rows]
        for m, other in enumerate(others):
            at = (k ^ (m + 1)) * rows
            total = total + other[:, at : at + rows]
        positives = jnp.maximum(total[5:6], 1.0)
        if k == 0:
            contrast = (1.0 - total[4:5] / positives) / temp_sup + jnp.log(total[0:1])
            relation = (1.0 - total[3:4] / total[2:3]) / temp_student + jnp.log(total[1:2])
            both = jnp.concatenate([contrast, relation] + [jnp.zeros((6, rows), jnp.float32)], axis=0)
            loss_ref[...] = jnp.broadcast_to(jnp.sum(both, axis=1, keepdims=True), (8, rows))
        factors = jnp.concatenate(
            [
                (1.0 / temp_sup) / total[0:1],
                (1.0 / temp_student) / total[1:2],
                (1.0 / temp_student) / total[2:3],
                (1.0 / temp_sup) / positives,
                jnp.zeros((rows - 4, rows), jnp.float32),
            ],
            axis=0,
        )
        key_ref[k * rows : (k + 1) * rows, :] = jnp.transpose(factors)
    low = lax.broadcasted_iota(jnp.int32, (8, rows), 0)
    for i in range(quarter):
        for dc in range(2):
            total = jnp.zeros((8, rows), jnp.float32)
            for h in range(groups // 2):
                for qq in range(2):
                    source = (h * 2 + (c ^ dc)) * members + (q * 2 + qq) * quarter + (r ^ i)
                    total = total + received_ref[pl.ds(pl.multiple_of(source * 8, 8), 8), :]
            kind = low & 3
            factors = jnp.where(
                kind == 3,
                (1.0 / temp_sup) / jnp.maximum(total, 1.0),
                jnp.where(kind == 0, 1.0 / temp_sup, 1.0 / temp_student) / total,
            )
            turned = jnp.concatenate([factors[4:8], factors[0:4]], axis=0)
            near = jnp.where(p == 0, factors, turned)
            far = jnp.where(p == 0, turned, factors)
            for slot, value in enumerate((near, far)):
                at = ((i * 2 + slot) * 2 + dc) * rows
                anchor_ref[:, at : at + rows] = value


def grad_kernel(tiles, rows, k, n_blocks, *refs):
    label_ref, key_ref, anchor_stats_ref = refs[:3]
    rest = refs[3:]
    similar, weights, labels, units = (rest[i * tiles : (i + 1) * tiles] for i in range(4))
    out_ref = rest[4 * tiles]
    row_at = lax.broadcasted_iota(jnp.int32, (rows, rows), 0)
    lane_at = lax.broadcasted_iota(jnp.int32, (rows, rows), 1)
    sup_key, rel_key, teacher_key, pos_key = (key_ref[:, i : i + 1] for i in range(4))
    total = None
    for i in range(tiles):
        row_parts, column_parts = [], []
        for n in range(n_blocks):
            across = slice(n * rows, (n + 1) * rows)
            at = (i * n_blocks + n) * rows
            sup_all, rel_all, teacher_all, pos_all = (
                anchor_stats_ref[j : j + 1, at : at + rows] for j in range(4)
            )
            same_block = key_id(k) == anchor_id((i * n_blocks + n) // 2, n % 2)
            distinct = row_at != lane_at - jnp.where(same_block, 0, rows)
            rel_exp = jnp.where(
                distinct, jnp.exp((similar[i][:, across] - 1.0) / temp_student), 0.0
            )
            sup_exp = rel_exp * rel_exp
            weight = weights[i][:, across]
            same = label_ref[...] == labels[i][0:1, across]
            positive = jnp.where(jnp.logical_and(same, distinct), 1.0, 0.0)
            row_parts.append(
                (
                    (sup_exp * sup_key - positive * pos_key)
                    + (rel_exp * rel_key - weight * teacher_key)
                ).astype(jnp.bfloat16)
            )
            column_parts.append(
                (
                    (sup_exp * sup_all - positive * pos_all)
                    + (rel_exp * rel_all - weight * teacher_all)
                ).astype(jnp.bfloat16)
            )
        both = jnp.concatenate(
            [jnp.concatenate(row_parts, axis=1), jnp.concatenate(column_parts, axis=1)], axis=0
        )
        part = jnp.dot(both, units[i][...], preferred_element_type=jnp.float32)
        total = part if total is None else total + part
    grad = total[0:rows] + total[rows : 2 * rows]
    if k == 0:
        out_ref[...] = grad
        return
    top = jnp.maximum(jnp.max(jnp.abs(grad), axis=1, keepdims=True), 2.0**-90)
    power = jnp.floor(jnp.log2(top))
    scaled = jnp.clip(jnp.floor(grad * jnp.exp2(14.0 - power) + 0.5), -32767.0, 32767.0)
    out_ref[0:rows, :] = scaled.astype(jnp.int32).astype(jnp.int16)
    out_ref[rows : rows + PAD, :] = jnp.zeros((PAD, out_ref.shape[1]), jnp.int16)
    powers = jnp.transpose(jnp.broadcast_to(power, (rows, rows)))[0:PAD]
    out_ref[rows : rows + PAD, 0:rows] = powers.astype(jnp.int32).astype(jnp.int16)


def final_kernel(student_ref, own_ref, *refs):
    out_ref = refs[-1]
    rows = own_ref.shape[0]
    grad = own_ref[...]
    for ref in refs[:-1]:
        powers = ref[rows : rows + PAD, 0:rows].astype(jnp.int32).astype(jnp.float32)
        scale = jnp.exp2(column_of(powers[0:1])[:, 0:1] - 14.0)
        grad = grad + ref[0:rows, :].astype(jnp.int32).astype(jnp.float32) * scale
    values = student_ref[...].astype(jnp.float32)
    scaling = lax.rsqrt(jnp.sum(values * values, axis=1, keepdims=True) + epsilon)
    unit = values * scaling
    along = jnp.sum(unit * grad, axis=1, keepdims=True)
    out_ref[...] = scaling * (grad - unit * along)


def body(student, teacher, labels):
    rows, width = student.shape
    groups, members = lax.axis_size("grp"), lax.axis_size("dev")
    halves, quarter = groups // 2, members // 4
    h, c, p, q, r = place()
    inner = p != q
    cross = [
        (d, d ^ (3 * quarter)) for d in range(members) if (d // (2 * quarter)) != (d // quarter) % 2
    ]

    digits = jnp.stack([labels // 256, labels % 256]).astype(jnp.bfloat16)
    tail = jnp.pad(digits, ((0, PAD - 2), (0, width - rows)))
    own = (student, jnp.concatenate([teacher, tail], axis=0))

    def both(move, block):
        return tuple(move(part) for part in block)

    near = both(lambda v: swapped(v, "dev", quarter), own)
    crossed = both(lambda v: lax.ppermute(v, "dev", cross), own)
    keys = [own, near]
    for bit in bits_of(halves):
        keys = keys + [both(lambda v: swapped(v, "grp", 2 * bit), item) for item in keys]
    far = both(lambda v: lax.ppermute(v, "dev", cross), near)
    anchors = [
        tuple(jnp.where(inner, a, b) for a, b in zip(crossed, own)),
        tuple(jnp.where(inner, a, b) for a, b in zip(far, near)),
    ]
    for bit in bits_of(quarter):
        anchors = anchors + [both(lambda v: swapped(v, "dev", bit), item) for item in anchors]
    late = len(anchors) - 1
    pairs = [(item, both(lambda v: swapped(v, "grp", 1), item)) for item in anchors[:late]]

    key_count, pair_count = len(keys), len(anchors)
    key_rows = key_count * rows
    f32 = functools.partial(jax.ShapeDtypeStruct, dtype=jnp.float32)
    b16 = functools.partial(jax.ShapeDtypeStruct, dtype=jnp.bfloat16)

    key_unit, key_teacher, key_label = call(
        functools.partial(keys_kernel, key_count, rows),
        (b16((key_rows, width)), b16((key_rows, width)), f32((key_rows, rows))),
        [k[0] for k in keys] + [k[1] for k in keys],
        flops=8 * key_rows * width,
        name="keys",
    )
    units, similar, weights, anchor_labels = [], [], [], []
    stats = None
    n_blocks, tiles = 2 * GROUP, pair_count // GROUP
    for i in range(tiles):
        last = i == tiles - 1
        if last:
            stats, held = lax.optimization_barrier((stats, anchors[late][0]))
            anchors[late] = (held, anchors[late][1])
            pairs.append((anchors[late], both(lambda v: swapped(v, "grp", 1), anchors[late])))
        chosen = [item for pair in pairs[i * GROUP : (i + 1) * GROUP] for item in pair]
        outs = call(
            functools.partial(tile_kernel, key_count, rows, i, n_blocks, last),
            (
                b16((n_blocks * rows, width)),
                f32((key_rows, n_blocks * rows)),
                f32((key_rows, n_blocks * rows)),
                f32((8, n_blocks * rows)),
                f32((key_rows, rows)),
            )
            + ((f32((8, key_rows)),) if last else ()),
            [key_unit, key_teacher, key_label]
            + [item[0] for item in chosen]
            + [item[1] for item in chosen]
            + ([] if stats is None else [stats]),
            flops=4 * key_rows * n_blocks * rows * width,
            name="tile",
        )
        for held, value in zip((units, similar, weights, anchor_labels), outs[:4]):
            held.append(value)
        stats = outs[4]
    sums = outs[5]

    others = []
    for k in range(1, key_count):
        mask = (k // 2) * 2 * members + (k % 2) * quarter
        total = groups * members
        others.append(lax.ppermute(sums, AXES, [(i, i ^ mask) for i in range(total)]))
    payload = call(
        functools.partial(payload_kernel, halves, members, rows),
        f32((groups * members * 8, rows)),
        [sums],
        name="payload",
    )
    received = lax.all_to_all(payload, AXES, 0, 0, tiled=True)
    anchor_stats, key_stats, loss = call(
        functools.partial(merge_kernel, (groups, members, key_count), rows),
        (f32((8, members * rows)), f32((key_rows, rows)), f32((8, rows))),
        [received, sums] + others,
        name="merge",
    )

    def grads(k, key_stats):
        blocks = {i: ((rows, rows), lambda step: (k, 0)) for i in (0, 1)}
        for i in range(2 * tiles):
            blocks[3 + i] = ((rows, n_blocks * rows), lambda step: (k, 0))
        operands = [key_label, key_stats, anchor_stats] + similar + weights + anchor_labels + units
        return call(
            functools.partial(grad_kernel, tiles, rows, k, n_blocks),
            f32((rows, width)) if k == 0 else jax.ShapeDtypeStruct((rows + PAD, width), jnp.int16),
            operands,
            flops=4 * rows * members * rows * width,
            name="grads",
            blocks=blocks,
        )

    parts = []
    for k in range(key_count - 1, -1, -1):
        part = grads(k, key_stats)
        if k:
            key_stats, part = lax.optimization_barrier((key_stats, part))
            mask = (k // 2) * 2 * members + (k % 2) * quarter
            part = lax.ppermute(part, AXES, [(i, i ^ mask) for i in range(groups * members)])
        parts.append(part)
    loss, parts[0], parts[-1] = lax.optimization_barrier((loss, parts[0], parts[-1]))
    shared = lax.all_to_all(
        jnp.broadcast_to(loss[None], (groups * members, 8, rows)).reshape(-1, rows), AXES, 0, 0, tiled=True
    ).reshape(groups * members, 8, rows)
    losses = jnp.sum(shared[:, 0:2, 0], axis=0) / (groups * members * rows)
    shares = [student] + parts[::-1]
    feature_grad = call(
        final_kernel,
        f32((rows, width)),
        shares,
        flops=8 * rows * width,
        name="final",
    )
    return (losses[0], losses[1], feature_grad)


def solution(mesh):
    placed = (P(AXES, None), P(AXES, None), P(AXES))
    return jax.shard_map(
        body,
        mesh=mesh,
        in_specs=placed,
        out_specs=(P(), P(), P(AXES, None)),
        check_vma=False,
    )
```

```python
import functools

import jax
import jax.numpy as jnp
from jax import lax
from jax.experimental import pallas as pl
from jax.experimental.pallas import tpu as pltpu
from jax.sharding import PartitionSpec as P

temp_sup = 0.1
temp_student = 0.2
temp_teacher = 0.05
epsilon = 1e-06

AXES = ("grp", "dev")
GROUP = 2
PAD = 16
VMEM_LIMIT = 63 * 1024 * 1024


def swapped(value, axis, mask):
    size = lax.axis_size(axis)
    return lax.ppermute(value, axis, [(i, i ^ mask) for i in range(size)])


def bits_of(size):
    return [1 << i for i in range(size.bit_length() - 1)]


def unit_of(raw):
    values = raw.astype(jnp.float32)
    scaling = lax.rsqrt(jnp.sum(values * values, axis=1, keepdims=True) + epsilon)
    return (values * scaling).astype(jnp.bfloat16)


def label_row(block, rows):
    tail = block[2 * rows : 2 * rows + PAD, 0:rows].astype(jnp.float32)
    return tail[0:1] * 256.0 + tail[1:2]


def column_of(row):
    rows = row.shape[1]
    return jnp.transpose(jnp.broadcast_to(row, (rows, rows)))


def inner_rows(left, right):
    return lax.dot_general(
        left, right, (((1,), (1,)), ((), ())), preferred_element_type=jnp.float32
    )


def call(kernel, out_shape, operands, flops=0, name=None, blocks=None):
    def spec(shape, given):
        if given is None:
            return pl.BlockSpec(shape, lambda step: (0, 0))
        return pl.BlockSpec(*given)

    many = isinstance(out_shape, (tuple, list))
    shapes = tuple(out_shape) if many else (out_shape,)
    out_specs = tuple(spec(item.shape, None) for item in shapes)
    moved = sum(item.size * item.dtype.itemsize for item in operands)
    return pl.pallas_call(
        kernel,
        out_shape=shapes if many else out_shape,
        grid=(1,),
        in_specs=[spec(item.shape, (blocks or {}).get(i)) for i, item in enumerate(operands)],
        out_specs=out_specs if many else out_specs[0],
        name=name,
        cost_estimate=pl.CostEstimate(flops=flops, bytes_accessed=moved, transcendentals=0),
        compiler_params=pltpu.CompilerParams(vmem_limit_bytes=VMEM_LIMIT),
    )(*operands)


def place():
    group, member = lax.axis_index("grp"), lax.axis_index("dev")
    quarter = lax.axis_size("dev") // 4
    return (
        group // 2,
        group % 2,
        member // (2 * quarter),
        (member // quarter) % 2,
        member % quarter,
    )


def key_id(k):
    h, c, p, q, r = place()
    members = lax.axis_size("dev")
    return ((h ^ (k // 2)) * 2 + c) * members + (p * 2 + (q ^ (k % 2))) * (members // 4) + r


def anchor_id(i, dc):
    h, c, p, q, r = place()
    members = lax.axis_size("dev")
    return (h * 2 + (c ^ dc)) * members + (q * 2 + (p ^ (i % 2))) * (members // 4) + (r ^ (i // 2))


def keys_kernel(count, rows, *refs):
    blocks = refs[:count]
    unit_ref, teacher_ref, label_ref = refs[count:]
    for k in range(count):
        place = slice(k * rows, (k + 1) * rows)
        unit_ref[place, :] = unit_of(blocks[k][0:rows, :])
        teacher_ref[place, :] = unit_of(blocks[k][rows : 2 * rows, :])
        label_ref[place, :] = column_of(label_row(blocks[k], rows))


def tile_kernel(count, rows, i, n_blocks, last, *refs):
    unit_ref, teacher_ref, label_ref = refs[:3]
    blocks, rest = refs[3 : 3 + n_blocks], refs[3 + n_blocks :]
    first = i == 0
    if not first:
        old_ref, rest = rest[0], rest[1:]
    anchor_ref, similar_ref, weight_ref, anchor_label_ref, stats_ref = rest[:5]
    teacher_units = []
    for n in range(n_blocks):
        across = slice(n * rows, (n + 1) * rows)
        anchor_ref[across, :] = unit_of(blocks[n][0:rows, :])
        teacher_units.append(unit_of(blocks[n][rows : 2 * rows, :]))
        anchor_label_ref[:, across] = jnp.broadcast_to(label_row(blocks[n], rows), (8, rows))
    similar_ref[...] = inner_rows(unit_ref[...], anchor_ref[...])
    weight_ref[...] = inner_rows(teacher_ref[...], jnp.concatenate(teacher_units, axis=0))
    row_at = lax.broadcasted_iota(jnp.int32, (rows, rows), 0)
    lane_at = lax.broadcasted_iota(jnp.int32, (rows, rows), 1)
    for k in range(count):
        down = slice(k * rows, (k + 1) * rows)
        totals = [jnp.zeros((rows, rows), jnp.float32)] * 6
        for n in range(n_blocks):
            across = slice(n * rows, (n + 1) * rows)
            similar = similar_ref[down, across]
            same_block = key_id(k) == anchor_id((i * n_blocks + n) // 2, n % 2)
            distinct = row_at != lane_at - jnp.where(same_block, 0, rows)
            rel_exp = jnp.where(distinct, jnp.exp((similar - 1.0) / temp_student), 0.0)
            weight = jnp.where(
                distinct, jnp.exp((weight_ref[down, across] - 1.0) / temp_teacher), 0.0
            )
            weight_ref[down, across] = weight
            same = label_ref[down, :] == anchor_label_ref[0:1, across]
            positive = jnp.where(jnp.logical_and(same, distinct), 1.0, 0.0)
            terms = (
                rel_exp * rel_exp,
                rel_exp,
                weight,
                weight * similar,
                positive * similar,
                positive,
            )
            totals = [total + term for total, term in zip(totals, terms)]
        stats = jnp.zeros((rows, rows), jnp.float32)
        for j, total in enumerate(totals):
            stats = jnp.where(lane_at == j, jnp.sum(total, axis=1, keepdims=True), stats)
        if not first:
            stats = stats + old_ref[down, :]
        stats_ref[down, :] = stats
        if last:
            rest[5][:, down] = jnp.transpose(stats)[0:8, :]


def payload_kernel(halves, members, rows, sums_ref, out_ref):
    h, _, _, q, _ = place()
    for half in range(halves):
        both = []
        for other in range(2):
            block = (half ^ h) * 2 + (other ^ q)
            values = sums_ref[:, pl.ds(pl.multiple_of(block * rows, rows), rows)]
            both += [values[0:3], values[5:6]]
        tile = jnp.concatenate(both, axis=0)
        for d in range(2 * members):
            at = (half * 2 * members + d) * 8
            out_ref[at : at + 8, :] = tile


def merge_kernel(dims, rows, *refs):
    groups, members, keys = dims
    received_ref, own_ref = refs[:2]
    others = refs[2 : 1 + keys]
    anchor_ref, key_ref, loss_ref = refs[1 + keys :]
    _, c, p, q, r = place()
    quarter = members // 4
    for k in range(keys):
        total = own_ref[:, k * rows : (k + 1) * rows]
        for m, other in enumerate(others):
            at = (k ^ (m + 1)) * rows
            total = total + other[:, at : at + rows]
        positives = jnp.maximum(total[5:6], 1.0)
        if k == 0:
            contrast = (1.0 - total[4:5] / positives) / temp_sup + jnp.log(total[0:1])
            relation = (1.0 - total[3:4] / total[2:3]) / temp_student + jnp.log(total[1:2])
            both = jnp.concatenate([contrast, relation] + [jnp.zeros((6, rows), jnp.float32)], axis=0)
            loss_ref[...] = jnp.broadcast_to(jnp.sum(both, axis=1, keepdims=True), (8, rows))
        factors = jnp.concatenate(
            [
                (1.0 / temp_sup) / total[0:1],
                (1.0 / temp_student) / total[1:2],
                (1.0 / temp_student) / total[2:3],
                (1.0 / temp_sup) / positives,
                jnp.zeros((rows - 4, rows), jnp.float32),
            ],
            axis=0,
        )
        key_ref[k * rows : (k + 1) * rows, :] = jnp.transpose(factors)
    low = lax.broadcasted_iota(jnp.int32, (8, rows), 0)
    for i in range(quarter):
        for dc in range(2):
            total = jnp.zeros((8, rows), jnp.float32)
            for h in range(groups // 2):
                for qq in range(2):
                    source = (h * 2 + (c ^ dc)) * members + (q * 2 + qq) * quarter + (r ^ i)
                    total = total + received_ref[pl.ds(pl.multiple_of(source * 8, 8), 8), :]
            kind = low & 3
            factors = jnp.where(
                kind == 3,
                (1.0 / temp_sup) / jnp.maximum(total, 1.0),
                jnp.where(kind == 0, 1.0 / temp_sup, 1.0 / temp_student) / total,
            )
            turned = jnp.concatenate([factors[4:8], factors[0:4]], axis=0)
            near = jnp.where(p == 0, factors, turned)
            far = jnp.where(p == 0, turned, factors)
            for slot, value in enumerate((near, far)):
                at = ((i * 2 + slot) * 2 + dc) * rows
                anchor_ref[:, at : at + rows] = value


def grad_kernel(tiles, rows, chosen, n_blocks, *refs):
    label_ref, key_ref, anchor_stats_ref = refs[:3]
    rest = refs[3:]
    similar, weights, labels, units = (rest[i * tiles : (i + 1) * tiles] for i in range(4))
    outs = rest[4 * tiles :]
    row_at = lax.broadcasted_iota(jnp.int32, (rows, rows), 0)
    lane_at = lax.broadcasted_iota(jnp.int32, (rows, rows), 1)
    total = None
    for i in range(tiles):
        lines = []
        for j, k in enumerate(chosen):
            down = slice(j * rows, (j + 1) * rows)
            sup_key, rel_key, teacher_key, pos_key = (key_ref[down, f : f + 1] for f in range(4))
            row_parts, column_parts = [], []
            for n in range(n_blocks):
                across = slice(n * rows, (n + 1) * rows)
                at = (i * n_blocks + n) * rows
                sup_all, rel_all, teacher_all, pos_all = (
                    anchor_stats_ref[f : f + 1, at : at + rows] for f in range(4)
                )
                same_block = key_id(k) == anchor_id((i * n_blocks + n) // 2, n % 2)
                distinct = row_at != lane_at - jnp.where(same_block, 0, rows)
                rel_exp = jnp.where(
                    distinct, jnp.exp((similar[i][down, across] - 1.0) / temp_student), 0.0
                )
                sup_exp = rel_exp * rel_exp
                weight = weights[i][down, across]
                same = label_ref[down, :] == labels[i][0:1, across]
                positive = jnp.where(jnp.logical_and(same, distinct), 1.0, 0.0)
                row_parts.append(
                    (
                        (sup_exp * sup_key - positive * pos_key)
                        + (rel_exp * rel_key - weight * teacher_key)
                    ).astype(jnp.bfloat16)
                )
                column_parts.append(
                    (
                        (sup_exp * sup_all - positive * pos_all)
                        + (rel_exp * rel_all - weight * teacher_all)
                    ).astype(jnp.bfloat16)
                )
            lines += [jnp.concatenate(row_parts, axis=1), jnp.concatenate(column_parts, axis=1)]
        part = jnp.dot(
            jnp.concatenate(lines, axis=0), units[i][...], preferred_element_type=jnp.float32
        )
        total = part if total is None else total + part
    for j, k in enumerate(chosen):
        at = 2 * j * rows
        grad = total[at : at + rows] + total[at + rows : at + 2 * rows]
        out_ref = outs[j]
        if k == 0:
            out_ref[...] = grad
            continue
        top = jnp.maximum(jnp.max(jnp.abs(grad), axis=1, keepdims=True), 2.0**-90)
        power = jnp.floor(jnp.log2(top))
        scaled = jnp.clip(jnp.floor(grad * jnp.exp2(14.0 - power) + 0.5), -32767.0, 32767.0)
        out_ref[0:rows, :] = scaled.astype(jnp.int32).astype(jnp.int16)
        out_ref[rows : rows + PAD, :] = jnp.zeros((PAD, out_ref.shape[1]), jnp.int16)
        powers = jnp.transpose(jnp.broadcast_to(power, (rows, rows)))[0:PAD]
        out_ref[rows : rows + PAD, 0:rows] = powers.astype(jnp.int32).astype(jnp.int16)


def final_kernel(student_ref, own_ref, *refs):
    out_ref = refs[-1]
    rows = own_ref.shape[0]
    grad = own_ref[...]
    for ref in refs[:-1]:
        powers = ref[rows : rows + PAD, 0:rows].astype(jnp.int32).astype(jnp.float32)
        scale = jnp.exp2(column_of(powers[0:1])[:, 0:1] - 14.0)
        grad = grad + ref[0:rows, :].astype(jnp.int32).astype(jnp.float32) * scale
    values = student_ref[...].astype(jnp.float32)
    scaling = lax.rsqrt(jnp.sum(values * values, axis=1, keepdims=True) + epsilon)
    unit = values * scaling
    along = jnp.sum(unit * grad, axis=1, keepdims=True)
    out_ref[...] = scaling * (grad - unit * along)


def ordered(items, at, value):
    first, value = lax.optimization_barrier((items[at], value))
    return items[:at] + [first] + items[at + 1 :], value


def body(student, teacher, labels):
    rows, width = student.shape
    groups, members = lax.axis_size("grp"), lax.axis_size("dev")
    halves, quarter = groups // 2, members // 4
    h, c, p, q, r = place()
    inner = p != q
    cross = [
        (d, d ^ (3 * quarter)) for d in range(members) if (d // (2 * quarter)) != (d // quarter) % 2
    ]

    digits = jnp.stack([labels // 256, labels % 256]).astype(jnp.bfloat16)
    tail = jnp.pad(digits, ((0, PAD - 2), (0, width - rows)))
    own = jnp.concatenate([student, teacher, tail], axis=0)

    near = swapped(own, "dev", quarter)
    crossed = lax.ppermute(own, "dev", cross)
    keys = [own, near]
    for bit in bits_of(halves):
        keys = keys + [swapped(item, "grp", 2 * bit) for item in keys]
    far = lax.ppermute(near, "dev", cross)
    keys, far = ordered(keys, 2, far)
    anchors = [jnp.where(inner, crossed, own), jnp.where(inner, far, near)]
    for bit in bits_of(quarter):
        anchors = anchors + [swapped(item, "dev", bit) for item in anchors]
    late = len(anchors) - 1
    keys, anchors[late - 1] = ordered(keys, len(keys) - 1, anchors[late - 1])
    pairs = [(item, swapped(item, "grp", 1)) for item in anchors[:late]]

    key_count, pair_count = len(keys), len(anchors)
    key_rows = key_count * rows
    f32 = functools.partial(jax.ShapeDtypeStruct, dtype=jnp.float32)
    b16 = functools.partial(jax.ShapeDtypeStruct, dtype=jnp.bfloat16)

    key_unit, key_teacher, key_label = call(
        functools.partial(keys_kernel, key_count, rows),
        (b16((key_rows, width)), b16((key_rows, width)), f32((key_rows, rows))),
        keys,
        flops=8 * key_rows * width,
        name="keys",
    )
    units, similar, weights, anchor_labels = [], [], [], []
    stats = None
    n_blocks, tiles = 2 * GROUP, pair_count // GROUP
    for i in range(tiles):
        last = i == tiles - 1
        if last:
            stats, anchors[late] = lax.optimization_barrier((stats, anchors[late]))
            pairs.append((anchors[late], swapped(anchors[late], "grp", 1)))
        chosen = [item for pair in pairs[i * GROUP : (i + 1) * GROUP] for item in pair]
        outs = call(
            functools.partial(tile_kernel, key_count, rows, i, n_blocks, last),
            (
                b16((n_blocks * rows, width)),
                f32((key_rows, n_blocks * rows)),
                f32((key_rows, n_blocks * rows)),
                f32((8, n_blocks * rows)),
                f32((key_rows, rows)),
            )
            + ((f32((8, key_rows)),) if last else ()),
            [key_unit, key_teacher, key_label]
            + chosen
            + ([] if stats is None else [stats]),
            flops=4 * key_rows * n_blocks * rows * width,
            name="tile",
        )
        for held, value in zip((units, similar, weights, anchor_labels), outs[:4]):
            held.append(value)
        stats = outs[4]
    sums = outs[5]

    others = []
    for k in range(1, key_count):
        mask = (k // 2) * 2 * members + (k % 2) * quarter
        total = groups * members
        others.append(lax.ppermute(sums, AXES, [(i, i ^ mask) for i in range(total)]))
    payload = call(
        functools.partial(payload_kernel, halves, members, rows),
        f32((groups * members * 8, rows)),
        [sums],
        name="payload",
    )
    received = lax.all_to_all(payload, AXES, 0, 0, tiled=True)
    anchor_stats, key_stats, loss = call(
        functools.partial(merge_kernel, (groups, members, key_count), rows),
        (f32((8, members * rows)), f32((key_rows, rows)), f32((8, rows))),
        [received, sums] + others,
        name="merge",
    )

    def grads(which, key_stats):
        chosen = (2 * which, 2 * which + 1)
        blocks = {i: ((2 * rows, rows), lambda step: (which, 0)) for i in (0, 1)}
        for i in range(2 * tiles):
            blocks[3 + i] = ((2 * rows, n_blocks * rows), lambda step: (which, 0))
        operands = [key_label, key_stats, anchor_stats] + similar + weights + anchor_labels + units
        return call(
            functools.partial(grad_kernel, tiles, rows, chosen, n_blocks),
            [
                f32((rows, width)) if k == 0 else jax.ShapeDtypeStruct((rows + PAD, width), jnp.int16)
                for k in chosen
            ],
            operands,
            flops=8 * rows * members * rows * width,
            name="grads",
            blocks=blocks,
        )

    parts = [None] * key_count
    for which in range(key_count // 2 - 1, -1, -1):
        both = list(grads(which, key_stats))
        for j in (1, 0):
            k = 2 * which + j
            if k:
                mask = (k // 2) * 2 * members + (k % 2) * quarter
                if which:
                    key_stats, both[j] = lax.optimization_barrier((key_stats, both[j]))
                both[j] = lax.ppermute(both[j], AXES, [(i, i ^ mask) for i in range(groups * members)])
            parts[k] = both[j]
    loss, parts[-1], parts[0] = lax.optimization_barrier((loss, parts[-1], parts[0]))
    shared = lax.all_to_all(
        jnp.broadcast_to(loss[None], (groups * members, 8, rows)).reshape(-1, rows), AXES, 0, 0, tiled=True
    ).reshape(groups * members, 8, rows)
    losses = jnp.sum(shared[:, 0:2, 0], axis=0) / (groups * members * rows)
    shares = [student] + parts
    feature_grad = call(
        final_kernel,
        f32((rows, width)),
        shares,
        flops=8 * rows * width,
        name="final",
    )
    return (losses[0], losses[1], feature_grad)


def solution(mesh):
    placed = (P(AXES, None), P(AXES, None), P(AXES))
    return jax.shard_map(
        body,
        mesh=mesh,
        in_specs=placed,
        out_specs=(P(), P(), P(AXES, None)),
        check_vma=False,
    )
```

```python
import functools

import jax
import jax.numpy as jnp
from jax import lax
from jax.experimental import pallas as pl
from jax.experimental.pallas import tpu as pltpu
from jax.sharding import PartitionSpec as P

temp_sup = 0.1
temp_student = 0.2
temp_teacher = 0.05
epsilon = 1e-06

AXES = ("grp", "dev")
GROUP = 2
PAD = 16
VMEM_LIMIT = 63 * 1024 * 1024


def swapped(value, axis, mask):
    size = lax.axis_size(axis)
    return lax.ppermute(value, axis, [(i, i ^ mask) for i in range(size)])


def bits_of(size):
    return [1 << i for i in range(size.bit_length() - 1)]


def unit_of(raw):
    values = raw.astype(jnp.float32)
    scaling = lax.rsqrt(jnp.sum(values * values, axis=1, keepdims=True) + epsilon)
    return (values * scaling).astype(jnp.bfloat16)


def label_row(block, rows):
    tail = block[2 * rows : 2 * rows + PAD, 0:rows].astype(jnp.float32)
    return tail[0:1] * 256.0 + tail[1:2]


def column_of(row):
    rows = row.shape[1]
    return jnp.transpose(jnp.broadcast_to(row, (rows, rows)))


def inner_rows(left, right):
    return lax.dot_general(
        left, right, (((1,), (1,)), ((), ())), preferred_element_type=jnp.float32
    )


def call(kernel, out_shape, operands, flops=0, name=None, blocks=None, limit=VMEM_LIMIT):
    def spec(shape, given):
        if given is None:
            return pl.BlockSpec(shape, lambda step: (0, 0))
        return pl.BlockSpec(*given)

    many = isinstance(out_shape, (tuple, list))
    shapes = tuple(out_shape) if many else (out_shape,)
    out_specs = tuple(spec(item.shape, None) for item in shapes)
    moved = sum(item.size * item.dtype.itemsize for item in operands)
    return pl.pallas_call(
        kernel,
        out_shape=shapes if many else out_shape,
        grid=(1,),
        in_specs=[spec(item.shape, (blocks or {}).get(i)) for i, item in enumerate(operands)],
        out_specs=out_specs if many else out_specs[0],
        name=name,
        cost_estimate=pl.CostEstimate(flops=flops, bytes_accessed=moved, transcendentals=0),
        compiler_params=pltpu.CompilerParams(vmem_limit_bytes=limit),
    )(*operands)


def place():
    group, member = lax.axis_index("grp"), lax.axis_index("dev")
    quarter = lax.axis_size("dev") // 4
    return (
        group // 2,
        group % 2,
        member // (2 * quarter),
        (member // quarter) % 2,
        member % quarter,
    )


def key_id(k):
    h, c, p, q, r = place()
    members = lax.axis_size("dev")
    return ((h ^ (k // 2)) * 2 + c) * members + (p * 2 + (q ^ (k % 2))) * (members // 4) + r


def anchor_id(i, dc):
    h, c, p, q, r = place()
    members = lax.axis_size("dev")
    return (h * 2 + (c ^ dc)) * members + (q * 2 + (p ^ (i % 2))) * (members // 4) + (r ^ (i // 2))


def pack_kernel(rows, student_ref, teacher_ref, label_ref, out_ref):
    out_ref[0:rows, :] = student_ref[...]
    out_ref[rows : 2 * rows, :] = teacher_ref[...]
    out_ref[2 * rows : 2 * rows + PAD, :] = jnp.zeros((PAD, out_ref.shape[1]), out_ref.dtype)
    high = lax.shift_right_logical(label_ref[...], 8)
    low = label_ref[...] & 255
    at = lax.broadcasted_iota(jnp.int32, (PAD, rows), 0)
    digits = jnp.where(at == 0, high, jnp.where(at == 1, low, 0)).astype(jnp.float32)
    out_ref[2 * rows : 2 * rows + PAD, 0:rows] = digits.astype(out_ref.dtype)


def keys_kernel(count, rows, *refs):
    blocks = refs[:count]
    unit_ref, teacher_ref, label_ref = refs[count:]
    for k in range(count):
        place = slice(k * rows, (k + 1) * rows)
        unit_ref[place, :] = unit_of(blocks[k][0:rows, :])
        teacher_ref[place, :] = unit_of(blocks[k][rows : 2 * rows, :])
        label_ref[place, :] = column_of(label_row(blocks[k], rows))


def tile_kernel(count, rows, i, n_blocks, last, *refs):
    unit_ref, teacher_ref, label_ref = refs[:3]
    blocks, rest = refs[3 : 3 + n_blocks], refs[3 + n_blocks :]
    first = i == 0
    if not first:
        old_ref, rest = rest[0], rest[1:]
    anchor_ref, similar_ref, weight_ref, anchor_label_ref, stats_ref = rest[:5]
    teacher_units = []
    for n in range(n_blocks):
        across = slice(n * rows, (n + 1) * rows)
        anchor_ref[across, :] = unit_of(blocks[n][0:rows, :])
        teacher_units.append(unit_of(blocks[n][rows : 2 * rows, :]))
        anchor_label_ref[:, across] = jnp.broadcast_to(label_row(blocks[n], rows), (8, rows))
    similar_ref[...] = inner_rows(unit_ref[...], anchor_ref[...])
    weight_ref[...] = inner_rows(teacher_ref[...], jnp.concatenate(teacher_units, axis=0))
    row_at = lax.broadcasted_iota(jnp.int32, (rows, rows), 0)
    lane_at = lax.broadcasted_iota(jnp.int32, (rows, rows), 1)
    for k in range(count):
        down = slice(k * rows, (k + 1) * rows)
        totals = [jnp.zeros((rows, rows), jnp.float32)] * 6
        for n in range(n_blocks):
            across = slice(n * rows, (n + 1) * rows)
            similar = similar_ref[down, across]
            same_block = key_id(k) == anchor_id((i * n_blocks + n) // 2, n % 2)
            distinct = row_at != lane_at - jnp.where(same_block, 0, rows)
            rel_exp = jnp.where(distinct, jnp.exp((similar - 1.0) / temp_student), 0.0)
            weight = jnp.where(
                distinct, jnp.exp((weight_ref[down, across] - 1.0) / temp_teacher), 0.0
            )
            weight_ref[down, across] = weight
            same = label_ref[down, :] == anchor_label_ref[0:1, across]
            positive = jnp.where(jnp.logical_and(same, distinct), 1.0, 0.0)
            terms = (
                rel_exp * rel_exp,
                rel_exp,
                weight,
                weight * similar,
                positive * similar,
                positive,
            )
            totals = [total + term for total, term in zip(totals, terms)]
        stats = jnp.zeros((rows, rows), jnp.float32)
        for j, total in enumerate(totals):
            stats = jnp.where(lane_at == j, jnp.sum(total, axis=1, keepdims=True), stats)
        if not first:
            stats = stats + old_ref[down, :]
        stats_ref[down, :] = stats
        if last:
            rest[5][:, down] = jnp.transpose(stats)[0:8, :]


def payload_kernel(halves, members, rows, sums_ref, out_ref):
    h, _, _, q, _ = place()
    for half in range(halves):
        both = []
        for other in range(2):
            block = (half ^ h) * 2 + (other ^ q)
            values = sums_ref[:, pl.ds(pl.multiple_of(block * rows, rows), rows)]
            both += [values[0:3], values[5:6]]
        tile = jnp.concatenate(both, axis=0)
        for d in range(2 * members):
            at = (half * 2 * members + d) * 8
            out_ref[at : at + 8, :] = tile


def merge_kernel(dims, rows, *refs):
    groups, members, keys = dims
    received_ref, own_ref = refs[:2]
    others = refs[2 : 1 + keys]
    anchor_ref, key_ref, loss_ref = refs[1 + keys :]
    _, c, p, q, r = place()
    quarter = members // 4
    for k in range(keys):
        total = own_ref[:, k * rows : (k + 1) * rows]
        for m, other in enumerate(others):
            at = (k ^ (m + 1)) * rows
            total = total + other[:, at : at + rows]
        positives = jnp.maximum(total[5:6], 1.0)
        if k == 0:
            contrast = (1.0 - total[4:5] / positives) / temp_sup + jnp.log(total[0:1])
            relation = (1.0 - total[3:4] / total[2:3]) / temp_student + jnp.log(total[1:2])
            both = jnp.concatenate([contrast, relation] + [jnp.zeros((6, rows), jnp.float32)], axis=0)
            loss = jnp.broadcast_to(jnp.sum(both, axis=1, keepdims=True), (8, rows))
            for d in range(groups * members):
                loss_ref[d * 8 : d * 8 + 8, :] = loss
        factors = jnp.concatenate(
            [
                (1.0 / temp_sup) / total[0:1],
                (1.0 / temp_student) / total[1:2],
                (1.0 / temp_student) / total[2:3],
                (1.0 / temp_sup) / positives,
                jnp.zeros((rows - 4, rows), jnp.float32),
            ],
            axis=0,
        )
        key_ref[k * rows : (k + 1) * rows, :] = jnp.transpose(factors)
    low = lax.broadcasted_iota(jnp.int32, (8, rows), 0)
    for i in range(quarter):
        for dc in range(2):
            total = jnp.zeros((8, rows), jnp.float32)
            for h in range(groups // 2):
                for qq in range(2):
                    source = (h * 2 + (c ^ dc)) * members + (q * 2 + qq) * quarter + (r ^ i)
                    total = total + received_ref[pl.ds(pl.multiple_of(source * 8, 8), 8), :]
            kind = low & 3
            factors = jnp.where(
                kind == 3,
                (1.0 / temp_sup) / jnp.maximum(total, 1.0),
                jnp.where(kind == 0, 1.0 / temp_sup, 1.0 / temp_student) / total,
            )
            turned = jnp.concatenate([factors[4:8], factors[0:4]], axis=0)
            near = jnp.where(p == 0, factors, turned)
            far = jnp.where(p == 0, turned, factors)
            for slot, value in enumerate((near, far)):
                at = ((i * 2 + slot) * 2 + dc) * rows
                anchor_ref[:, at : at + rows] = value


def grad_kernel(tiles, rows, chosen, n_blocks, *refs):
    label_ref, key_ref, anchor_stats_ref = refs[:3]
    rest = refs[3:]
    similar, weights, labels, units = (rest[i * tiles : (i + 1) * tiles] for i in range(4))
    outs = rest[4 * tiles :]
    row_at = lax.broadcasted_iota(jnp.int32, (rows, rows), 0)
    lane_at = lax.broadcasted_iota(jnp.int32, (rows, rows), 1)
    total = None
    for i in range(tiles):
        lines = []
        for j, k in enumerate(chosen):
            down = slice(j * rows, (j + 1) * rows)
            sup_key, rel_key, teacher_key, pos_key = (key_ref[down, f : f + 1] for f in range(4))
            row_parts, column_parts = [], []
            for n in range(n_blocks):
                across = slice(n * rows, (n + 1) * rows)
                at = (i * n_blocks + n) * rows
                sup_all, rel_all, teacher_all, pos_all = (
                    anchor_stats_ref[f : f + 1, at : at + rows] for f in range(4)
                )
                same_block = key_id(k) == anchor_id((i * n_blocks + n) // 2, n % 2)
                distinct = row_at != lane_at - jnp.where(same_block, 0, rows)
                rel_exp = jnp.where(
                    distinct, jnp.exp((similar[i][down, across] - 1.0) / temp_student), 0.0
                )
                sup_exp = rel_exp * rel_exp
                weight = weights[i][down, across]
                same = label_ref[down, :] == labels[i][0:1, across]
                positive = jnp.where(jnp.logical_and(same, distinct), 1.0, 0.0)
                row_parts.append(
                    (
                        (sup_exp * sup_key - positive * pos_key)
                        + (rel_exp * rel_key - weight * teacher_key)
                    ).astype(jnp.bfloat16)
                )
                column_parts.append(
                    (
                        (sup_exp * sup_all - positive * pos_all)
                        + (rel_exp * rel_all - weight * teacher_all)
                    ).astype(jnp.bfloat16)
                )
            lines += [jnp.concatenate(row_parts, axis=1), jnp.concatenate(column_parts, axis=1)]
        part = jnp.dot(
            jnp.concatenate(lines, axis=0), units[i][...], preferred_element_type=jnp.float32
        )
        total = part if total is None else total + part
    for j, k in enumerate(chosen):
        at = 2 * j * rows
        grad = total[at : at + rows] + total[at + rows : at + 2 * rows]
        out_ref = outs[j]
        if k == 0:
            out_ref[...] = grad
            continue
        top = jnp.maximum(jnp.max(jnp.abs(grad), axis=1, keepdims=True), 2.0**-90)
        power = jnp.floor(jnp.log2(top))
        scaled = jnp.clip(jnp.floor(grad * jnp.exp2(14.0 - power) + 0.5), -32767.0, 32767.0)
        out_ref[0:rows, :] = scaled.astype(jnp.int32).astype(jnp.int16)
        out_ref[rows : rows + PAD, :] = jnp.zeros((PAD, out_ref.shape[1]), jnp.int16)
        powers = jnp.transpose(jnp.broadcast_to(power, (rows, rows)))[0:PAD]
        out_ref[rows : rows + PAD, 0:rows] = powers.astype(jnp.int32).astype(jnp.int16)


def final_kernel(student_ref, own_ref, *refs):
    out_ref = refs[-1]
    rows = own_ref.shape[0]
    grad = own_ref[...]
    for ref in refs[:-1]:
        powers = ref[rows : rows + PAD, 0:rows].astype(jnp.int32).astype(jnp.float32)
        scale = jnp.exp2(column_of(powers[0:1])[:, 0:1] - 14.0)
        grad = grad + ref[0:rows, :].astype(jnp.int32).astype(jnp.float32) * scale
    values = student_ref[...].astype(jnp.float32)
    scaling = lax.rsqrt(jnp.sum(values * values, axis=1, keepdims=True) + epsilon)
    unit = values * scaling
    along = jnp.sum(unit * grad, axis=1, keepdims=True)
    out_ref[...] = scaling * (grad - unit * along)


def ordered(items, at, value):
    first, value = lax.optimization_barrier((items[at], value))
    return items[:at] + [first] + items[at + 1 :], value


def body(student, teacher, labels):
    rows, width = student.shape
    groups, members = lax.axis_size("grp"), lax.axis_size("dev")
    halves, quarter = groups // 2, members // 4
    h, c, p, q, r = place()
    inner = p != q
    cross = [
        (d, d ^ (3 * quarter)) for d in range(members) if (d // (2 * quarter)) != (d // quarter) % 2
    ]

    own = call(
        functools.partial(pack_kernel, rows),
        jax.ShapeDtypeStruct((2 * rows + PAD, width), jnp.bfloat16),
        [student, teacher, labels.reshape(1, rows)],
        name="pack",
    )

    near = swapped(own, "dev", quarter)
    crossed = lax.ppermute(own, "dev", cross)
    keys = [own, near]
    for bit in bits_of(halves):
        keys = keys + [swapped(item, "grp", 2 * bit) for item in keys]
    far = lax.ppermute(near, "dev", cross)
    keys, far = ordered(keys, 2, far)
    anchors = [jnp.where(inner, crossed, own), jnp.where(inner, far, near)]
    for bit in bits_of(quarter):
        anchors = anchors + [swapped(item, "dev", bit) for item in anchors]
    late = len(anchors) - 1
    keys, anchors[late - 1] = ordered(keys, len(keys) - 1, anchors[late - 1])
    pairs = [(item, swapped(item, "grp", 1)) for item in anchors[:late]]

    key_count, pair_count = len(keys), len(anchors)
    key_rows = key_count * rows
    f32 = functools.partial(jax.ShapeDtypeStruct, dtype=jnp.float32)
    b16 = functools.partial(jax.ShapeDtypeStruct, dtype=jnp.bfloat16)

    key_unit, key_teacher, key_label = call(
        functools.partial(keys_kernel, key_count, rows),
        (b16((key_rows, width)), b16((key_rows, width)), f32((key_rows, rows))),
        keys,
        flops=8 * key_rows * width,
        name="keys",
    )
    units, similar, weights, anchor_labels = [], [], [], []
    stats = None
    n_blocks, tiles = 2 * GROUP, pair_count // GROUP
    for i in range(tiles):
        last = i == tiles - 1
        if last:
            stats, anchors[late] = lax.optimization_barrier((stats, anchors[late]))
            pairs.append((anchors[late], swapped(anchors[late], "grp", 1)))
        chosen = [item for pair in pairs[i * GROUP : (i + 1) * GROUP] for item in pair]
        outs = call(
            functools.partial(tile_kernel, key_count, rows, i, n_blocks, last),
            (
                b16((n_blocks * rows, width)),
                f32((key_rows, n_blocks * rows)),
                f32((key_rows, n_blocks * rows)),
                f32((8, n_blocks * rows)),
                f32((key_rows, rows)),
            )
            + ((f32((8, key_rows)),) if last else ()),
            [key_unit, key_teacher, key_label]
            + chosen
            + ([] if stats is None else [stats]),
            flops=4 * key_rows * n_blocks * rows * width,
            name="tile",
        )
        for held, value in zip((units, similar, weights, anchor_labels), outs[:4]):
            held.append(value)
        stats = outs[4]
    sums = outs[5]

    others = []
    for k in range(1, key_count):
        mask = (k // 2) * 2 * members + (k % 2) * quarter
        total = groups * members
        others.append(lax.ppermute(sums, AXES, [(i, i ^ mask) for i in range(total)]))
    payload = call(
        functools.partial(payload_kernel, halves, members, rows),
        f32((groups * members * 8, rows)),
        [sums],
        name="payload",
    )
    received = lax.all_to_all(payload, AXES, 0, 0, tiled=True)
    anchor_stats, key_stats, loss = call(
        functools.partial(merge_kernel, (groups, members, key_count), rows),
        (f32((8, members * rows)), f32((key_rows, rows)), f32((groups * members * 8, rows))),
        [received, sums] + others,
        name="merge",
    )

    def grads(which, key_stats):
        chosen = (2 * which, 2 * which + 1)
        blocks = {i: ((2 * rows, rows), lambda step: (which, 0)) for i in (0, 1)}
        for i in range(2 * tiles):
            blocks[3 + i] = ((2 * rows, n_blocks * rows), lambda step: (which, 0))
        operands = [key_label, key_stats, anchor_stats] + similar + weights + anchor_labels + units
        return call(
            functools.partial(grad_kernel, tiles, rows, chosen, n_blocks),
            [
                f32((rows, width)) if k == 0 else jax.ShapeDtypeStruct((rows + PAD, width), jnp.int16)
                for k in chosen
            ],
            operands,
            flops=8 * rows * members * rows * width,
            name="grads",
            blocks=blocks,
        )

    parts = [None] * key_count
    for which in range(key_count // 2 - 1, -1, -1):
        both = list(grads(which, key_stats))
        for j in (1, 0):
            k = 2 * which + j
            if k:
                mask = (k // 2) * 2 * members + (k % 2) * quarter
                if which:
                    key_stats, both[j] = lax.optimization_barrier((key_stats, both[j]))
                both[j] = lax.ppermute(both[j], AXES, [(i, i ^ mask) for i in range(groups * members)])
            parts[k] = both[j]
    loss, parts[-1], parts[0] = lax.optimization_barrier((loss, parts[-1], parts[0]))
    shared = lax.all_to_all(loss, AXES, 0, 0, tiled=True).reshape(groups * members, 8, rows)
    losses = jnp.sum(shared[:, 0:2, 0], axis=0) / (groups * members * rows)
    shares = [student] + parts
    feature_grad = call(
        final_kernel,
        f32((rows, width)),
        shares,
        flops=8 * rows * width,
        name="final",
        limit=VMEM_LIMIT // 4,
    )
    return (losses[0], losses[1], feature_grad)


def solution(mesh):
    placed = (P(AXES, None), P(AXES, None), P(AXES))
    return jax.shard_map(
        body,
        mesh=mesh,
        in_specs=placed,
        out_specs=(P(), P(), P(AXES, None)),
        check_vma=False,
    )
```
